512 devices in a mesh: seq: 64 (over y, z), head: 8 (over x, core).
Axes of the slice: x: 4, y: 4, z: 16, core: 2. Of those that a mesh axis runs over, the one named last changes fastest.
Arguments:
- head_input: bfloat16 [16384, 8192], P('seq', 'head'), may hold values from -6 to 6
- out_grad: bfloat16 [16384, 8192], P('seq', 'head'), may hold values from -6 to 6
- b_proj: bfloat16 [16384, 1024], P('seq', 'head'), may hold values from -6 to 6
- c_proj: bfloat16 [16384, 1024], P('seq', 'head'), may hold values from -6 to 6
- time_step: float32 [128, 16384], P('head', 'seq'), may hold values from 0.0005 to 0.0015
- decay_log: float32 [128], P('head'), may hold values from -7 to 4, as said below
- skip_gain: float32 [128], P('head'), may hold values from 0.5 to 1.5
- layer_input: bfloat16 [16384, 4096], P('seq', 'head'), may hold values from -6 to 6
Outputs:
- input_grad: bfloat16 [16384, 8192], P('seq', 'head')
- bc_grad: float32 [16384, 2048], P('seq', 'head')
- weight_grad: float32 [8, 256, 4096], P('head', 'seq')
The draws below stay inside these ranges and needn't reach their ends.
Inputs may be any that keep to these rules, and one draw needn't show every extreme that they name: decay_log is the logarithm of a positive rate of each head.
All inputs are finite; a program needn't handle non-finite values.
Results may differ from the reference program's by a relative error of at most 0.0064.
Values may be sent and summed in bfloat16 or wider, within the bound.
No kernel may reach another device: no remote copies, remote signals or barrier semaphores. Data moves between devices by JAX's collectives and lax.ppermute only.
A program may use at most 192 MiB of HBM per device.

```python
import math
import jax
import jax.numpy as jnp
from jax import lax

D = 4096
GROUP_HEADS = 16
HEAD_DIM = 64
STATE = 128
BLOCK = 256
GROUPS = 8
HEADS = 128
LENGTH = 16384


def draw_decay_log(key, part):
    key = jax.random.fold_in(key, 11)
    pick_key, fast_key, slow_key = jax.random.split(key, 3)
    fast_share = 0.5
    fast_heads = jax.random.bernoulli(pick_key, fast_share, (HEADS,))
    fast_rate = jnp.exp(jax.random.uniform(fast_key, (HEADS,), jnp.float32, math.log(1.0 / 50.0), math.log(1.0 / 30.0)))
    slow_rate = jnp.exp(jax.random.uniform(slow_key, (HEADS,), jnp.float32, math.log(0.3), 0.0)) * (math.log(10.0) / LENGTH)
    return jnp.log(jnp.where(fast_heads, fast_rate, slow_rate) / 0.001).astype(jnp.float32)


def level_of(own_key, extent, pieces, low, largest):
    def one(axis_at, shards_of):
        heights = jax.random.uniform(jax.random.fold_in(jax.random.fold_in(own_key, 6), axis_at), (shards_of,), jnp.float32, low / len(pieces), largest / len(pieces))
        return jnp.repeat(jnp.exp(heights), extent[axis_at] // shards_of).reshape((-1,) + (1,) * (len(extent) - axis_at - 1))

    loudness = one(*pieces[0])
    for cut in pieces[1:]:
        loudness = loudness * one(*cut)
    return loudness


def scatter_about(own_key, dims, spread, limit, cuts=(), dtype=jnp.bfloat16):
    gain = level_of(own_key, dims, cuts, -0.22, 0.18) if cuts else 1.0
    array = jax.random.normal(own_key, dims, jnp.float32) * spread * gain
    return jnp.minimum(jnp.maximum(array, -limit), limit).astype(dtype)


def setup_inputs(seed: int = 0) -> dict:
    key_list = jax.random.split(jax.random.key(seed), 9)
    return {
        "head_input": scatter_about(key_list[0], (LENGTH, HEADS * HEAD_DIM), 1.0, 6.0, ((0, 64), (1, 8))),
        "out_grad": scatter_about(key_list[1], (LENGTH, HEADS * HEAD_DIM), 1.0, 6.0, ((0, 64), (1, 8))),
        "b_proj": scatter_about(key_list[2], (LENGTH, GROUPS * STATE), 1.0, 6.0, ((0, 64), (1, 8))),
        "c_proj": scatter_about(key_list[3], (LENGTH, GROUPS * STATE), 1.0, 6.0, ((0, 64), (1, 8))),
        "time_step": jnp.clip(0.0005 + 0.000999999989 * jax.random.uniform(key_list[4], (HEADS, LENGTH), jnp.float32) ** level_of(key_list[4], (HEADS, LENGTH), ((0, 8), (1, 64)), -0.2, 0.2), 0.0005, 0.0015),
        "decay_log": draw_decay_log(jax.random.fold_in(key_list[8], 71), 0),
        "skip_gain": jnp.clip(0.5 + 1.0 * jax.random.uniform(key_list[6], (HEADS,), jnp.float32) ** level_of(key_list[6], (HEADS,), ((0, 8),), -0.2, 0.2), 0.5, 1.5),
        "layer_input": scatter_about(key_list[7], (LENGTH, D), 1.0, 6.0, ((0, 64), (1, 8))),
    }


def outer_rows(left, right):
    return lax.dot_general(left, right, (((0,), (0,)), ((), ())), preferred_element_type=jnp.float32)


def expand_heads(final_log, head_dim):
    return jnp.repeat(jnp.exp(final_log), head_dim)[:, None]


def block_terms(head_block, grad_block, step_block, decay_rates):
    log_decay = step_block * decay_rates[:, None]
    cumulative = jnp.cumsum(log_decay, axis=1)
    final_log = cumulative[:, -1]
    input_weight = jnp.exp(final_log[:, None] - cumulative) * step_block
    scaled_input = (head_block * input_weight.T[:, :, None]).astype(jnp.bfloat16)
    scaled_grad = (grad_block * jnp.exp(cumulative).T[:, :, None]).astype(jnp.bfloat16)
    return cumulative, final_log, input_weight, scaled_input, scaled_grad


def block_grads(head_block, grad_block, b_block, c_block, step_block, terms, start_state, end_state, skip_gain):
    cumulative, final_log, input_weight, scaled_input, scaled_grad = terms
    block_len = head_block.shape[0]
    scores = jnp.dot(c_block, b_block.T, preferred_element_type=jnp.float32)
    positions = jnp.arange(block_len)
    causal = positions[:, None] >= positions[None, :]
    gaps = cumulative[:, :, None] - cumulative[:, None, :]
    decay_matrix = jnp.where(causal, jnp.exp(jnp.where(causal, gaps, 0.0)), 0.0) * step_block[:, None, :]
    transfer = (scores[None] * decay_matrix).astype(jnp.bfloat16)
    inner_grad = jnp.einsum("hsr,shp->rhp", transfer.astype(jnp.float32), grad_block.astype(jnp.float32))
    pairs = jnp.einsum("shp,rhp->hsr", grad_block.astype(jnp.float32), head_block.astype(jnp.float32))
    mixed = jnp.sum(pairs * decay_matrix, axis=0).astype(jnp.bfloat16)
    start_low = start_state.astype(jnp.bfloat16)
    end_low = end_state.astype(jnp.bfloat16)
    carried = jnp.dot(b_block, end_low.T, preferred_element_type=jnp.float32).reshape(head_block.shape)
    carried = carried * input_weight.T[:, :, None]
    input_grad = (skip_gain[None, :, None] * grad_block + inner_grad + carried).astype(jnp.bfloat16)
    input_grad = input_grad.reshape(block_len, -1)
    grad_b = jnp.dot(mixed.T, c_block, preferred_element_type=jnp.float32)
    grad_b = grad_b + jnp.dot(scaled_input.reshape(block_len, -1), end_low, preferred_element_type=jnp.float32)
    grad_c = jnp.dot(mixed, b_block, preferred_element_type=jnp.float32)
    grad_c = grad_c + jnp.dot(scaled_grad.reshape(block_len, -1), start_low, preferred_element_type=jnp.float32)
    return input_grad, jnp.concatenate([grad_b, grad_c], axis=1)


def reference(head_input, out_grad, b_proj, c_proj, time_step, decay_log, skip_gain, layer_input):
    decay_rates = -jnp.exp(decay_log)
    blocks = LENGTH // BLOCK
    width = GROUP_HEADS * HEAD_DIM
    grads_x = []
    grads_bc = []
    weights = []
    for group in range(GROUPS):
        head_span = slice(group * GROUP_HEADS, (group + 1) * GROUP_HEADS)
        col_span = slice(group * width, (group + 1) * width)
        state_span = slice(group * STATE, (group + 1) * STATE)
        heads_all = head_input[:, col_span].reshape(blocks, BLOCK, GROUP_HEADS, HEAD_DIM)
        grads_all = out_grad[:, col_span].reshape(blocks, BLOCK, GROUP_HEADS, HEAD_DIM)
        b_all = b_proj[:, state_span].reshape(blocks, BLOCK, STATE)
        c_all = c_proj[:, state_span].reshape(blocks, BLOCK, STATE)
        steps_all = time_step[head_span].reshape(GROUP_HEADS, blocks, BLOCK).transpose(1, 0, 2)
        group_rates = decay_rates[head_span]
        group_skip = skip_gain[head_span]

        def first_pass(items):
            head_block, grad_block, b_block, c_block, step_block = items
            terms = block_terms(head_block, grad_block, step_block, group_rates)
            state_in = outer_rows(terms[3].reshape(BLOCK, -1), b_block)
            state_grad = outer_rows(terms[4].reshape(BLOCK, -1), c_block)
            return terms[1], state_in, state_grad

        finals, states_in, states_grad = lax.map(first_pass, (heads_all, grads_all, b_all, c_all, steps_all))
        zero_state = jnp.zeros((width, STATE), jnp.float32)

        def forward_step(carry, items):
            return expand_heads(items[0], HEAD_DIM) * carry + items[1], carry

        def backward_step(carry, items):
            return items[1] + expand_heads(items[0], HEAD_DIM) * carry, carry

        starts = lax.scan(forward_step, zero_state, (finals, states_in))[1]
        ends = lax.scan(backward_step, zero_state, (finals, states_grad), reverse=True)[1]

        def second_pass(items):
            head_block, grad_block, b_block, c_block, step_block, start_state, end_state = items
            terms = block_terms(head_block, grad_block, step_block, group_rates)
            return block_grads(head_block, grad_block, b_block, c_block, step_block, terms, start_state, end_state, group_skip)

        input_grad, bc_grad = lax.map(second_pass, (heads_all, grads_all, b_all, c_all, steps_all, starts, ends))
        input_grad = input_grad.reshape(LENGTH, width)
        bc_grad = bc_grad.reshape(LENGTH, 2 * STATE)
        bc_low = bc_grad.astype(jnp.bfloat16)
        weights.append(outer_rows(bc_low, layer_input) / LENGTH)
        grads_x.append(input_grad)
        grads_bc.append(bc_grad)
    return jnp.concatenate(grads_x, axis=1), jnp.concatenate(grads_bc, axis=1), jnp.stack(weights)
```

```python
import jax
import jax.numpy as jnp
from jax import lax
from jax.sharding import Mesh, PartitionSpec as P

Y, Z, X, CORE = 4, 16, 4, 2
BLOCK = 256
HEADS = 16
DIM = 64
STATE = 128
bf16 = jnp.bfloat16
f32 = jnp.float32


def rows_dot(left, right):
    return lax.dot_general(left, right, (((0,), (0,)), ((), ())), preferred_element_type=f32)


def to_chunks(state):
    return state.reshape(2, 64, 8, 128).transpose(2, 0, 1, 3).reshape(16, 64, 128)


def from_chunks(chunks):
    return chunks.reshape(8, 2, 64, 128).transpose(1, 2, 0, 3).reshape(128, 1024)


def pieces_of(value):
    high = value.astype(bf16)
    rest = value - high.astype(f32)
    mid = rest.astype(bf16)
    low = (rest - mid.astype(f32)).astype(bf16)
    return high, mid, low


def local(head_input, out_grad, b_proj, c_proj, time_step, decay_log, skip_gain, layer_input):
    everything = lax.all_gather(layer_input, ("y", "x", "core"))
    rates = -jnp.exp(decay_log)
    cum = jnp.cumsum(time_step * rates[:, None], axis=1)
    last = cum[:, -1]
    coef = jnp.exp(last[:, None] - cum) * time_step
    col_weight = jnp.repeat(coef.T, DIM, axis=1)
    grad_weight = jnp.repeat(jnp.exp(cum).T, DIM, axis=1)
    xs = (head_input * col_weight).astype(bf16)
    dys = (out_grad * grad_weight).astype(bf16)
    state_in = to_chunks(rows_dot(b_proj, xs))
    state_grad = to_chunks(rows_dot(c_proj, dys))
    lane_log = jnp.repeat(jnp.repeat(last, DIM).reshape(8, 1, 128), 2, axis=0)
    high, mid, low = pieces_of(lane_log)
    packed = jnp.concatenate(
        [state_in.astype(bf16), state_grad.astype(bf16), high, mid, low, jnp.zeros((16, 5, 128), bf16)], axis=1
    )
    got = lax.all_to_all(packed, "z", 0, 0, tiled=True)

    heads_three = head_input.reshape(BLOCK, HEADS, DIM)
    grads_three = out_grad.reshape(BLOCK, HEADS, DIM)
    scores = jnp.dot(c_proj, b_proj.T, preferred_element_type=f32)
    positions = jnp.arange(BLOCK)
    causal = positions[:, None] >= positions[None, :]
    gaps = cum[:, :, None] - cum[:, None, :]
    decay = jnp.where(causal, jnp.exp(jnp.where(causal, gaps, 0.0)), 0.0) * time_step[:, None, :]
    transfer = (scores[None] * decay).astype(bf16)
    inner = jnp.einsum("hsr,shp->rhp", transfer, grads_three, preferred_element_type=f32).reshape(BLOCK, -1)
    pairs = jnp.einsum("shp,rhp->hsr", grads_three, heads_three, preferred_element_type=f32)
    mixed = jnp.sum(pairs * decay, axis=0).astype(bf16)
    grad_b = jnp.dot(mixed.T, c_proj, preferred_element_type=f32)
    grad_c = jnp.dot(mixed, b_proj, preferred_element_type=f32)
    inner = inner + jnp.repeat(skip_gain, DIM)[None, :] * out_grad

    logs = jnp.sum(got[:, 128:131].astype(f32), axis=1, keepdims=True)
    fwd = got[:, :64].astype(f32)
    bwd = got[:, 64:128].astype(f32)
    decays = jnp.exp(logs)
    starts = [jnp.zeros((64, 128), f32)]
    for z in range(Z):
        starts.append(decays[z] * starts[-1] + fwd[z])
    ends = [jnp.zeros((64, 128), f32)]
    for z in reversed(range(Z)):
        ends.append(decays[z] * ends[-1] + bwd[z])
    row_log = jnp.sum(logs, axis=0)
    totals = jnp.concatenate([starts[-1], ends[-1], row_log, jnp.zeros((7, 128), f32)], axis=0)
    rows = lax.all_gather(totals, "y")
    here = lax.axis_index("y")
    row_decays = jnp.exp(rows[:, 128:129])
    carry = jnp.zeros((64, 128), f32)
    carry_end = jnp.zeros((64, 128), f32)
    for y in range(Y - 1):
        carry = jnp.where(y < here, row_decays[y] * carry + rows[y, :64], carry)
        up = Y - 1 - y
        carry_end = jnp.where(up > here, row_decays[up] * carry_end + rows[up, 64:128], carry_end)
    before = jnp.exp(jnp.cumsum(logs, axis=0) - logs)
    after = jnp.exp(row_log[None] - jnp.cumsum(logs, axis=0))
    start_all = jnp.stack(starts[:Z]) + before * carry[None]
    end_all = jnp.stack(ends[:Z][::-1]) + after * carry_end[None]
    back = jnp.concatenate([start_all.astype(bf16), end_all.astype(bf16)], axis=1)
    back = lax.all_to_all(back, "z", 0, 0, tiled=True)
    start_low = from_chunks(back[:, :64])
    end_low = from_chunks(back[:, 64:])

    grad_b = grad_b + lax.dot_general(xs, end_low, (((1,), (1,)), ((), ())), preferred_element_type=f32)
    grad_c = grad_c + lax.dot_general(dys, start_low, (((1,), (1,)), ((), ())), preferred_element_type=f32)
    bc_grad = jnp.concatenate([grad_b, grad_c], axis=1)
    bc_low = bc_grad.astype(bf16)
    shares = lax.all_to_all(bc_low.reshape(BLOCK, Y, 64).transpose(1, 0, 2), "y", 0, 0, tiled=True)
    carried = jnp.dot(b_proj, end_low, preferred_element_type=f32) * col_weight
    input_grad = (inner + carried).astype(bf16)

    term = jnp.einsum("ytr,ygtf->rgf", shares, everything.reshape(Y, X * CORE, BLOCK, 512), preferred_element_type=f32)
    term = term.astype(bf16).reshape(Z, 4, 4096)
    parts = lax.all_to_all(term, "z", 0, 0, tiled=True)
    weight = jnp.sum(parts.astype(f32), axis=0) / (BLOCK * Y * Z)
    return input_grad, bc_grad, weight[None]


def solution(mesh):
    fine = Mesh(mesh.devices.reshape(Y, Z, X, CORE), ("y", "z", "x", "core"))
    seq, head = ("y", "z"), ("x", "core")
    tokens = P(seq, head)
    in_specs = (tokens, tokens, tokens, tokens, P(head, seq), P(head), P(head), tokens)
    out_specs = (tokens, tokens, P(head, seq, None))
    return jax.shard_map(local, mesh=fine, in_specs=in_specs, out_specs=out_specs, check_vma=False)
```

```python
import jax
import jax.numpy as jnp
from jax import lax
from jax.experimental import pallas as pl
from jax.experimental.pallas import tpu as pltpu
from jax.sharding import Mesh, PartitionSpec as P

Y, ZH, ZM, ZL, X, CORE = 4, 4, 2, 2, 4, 2
TOKENS = 256
HEADS = 16
PAIRS = 8
STATE = 128
LANES = 128
WIDTH = 1024
NEAR = ZM * ZL
GROUPS = Y * ZH
PART = STATE // NEAR
HALF = PART // 2
bf16 = jnp.bfloat16
f32 = jnp.float32


def dot_tt(left, right):
    return lax.dot_general(left, right, (((0,), (0,)), ((), ())), preferred_element_type=f32)


def dot_nt(left, right):
    return lax.dot_general(left, right, (((1,), (1,)), ((), ())), preferred_element_type=f32)


def dot_nn(left, right):
    return lax.dot_general(left, right, (((1,), (0,)), ((), ())), preferred_element_type=f32)


def low_lanes():
    return lax.broadcasted_iota(jnp.int32, (1, LANES), 1) < 64


def spread(columns, first, k):
    return jnp.where(low_lanes(), columns[:, first + 2 * k : first + 2 * k + 1], columns[:, first + 2 * k + 1 : first + 2 * k + 2])


def log_rows(log):
    high = log.astype(bf16).astype(f32)
    mid = (log - high).astype(bf16).astype(f32)
    low = log - high - mid
    row = lax.broadcasted_iota(jnp.int32, (8, log.shape[1]), 0)
    rows = jnp.where(row == 0, high, jnp.where(row == 1, mid, jnp.where(row == 2, low, 0.0)))
    return rows.astype(bf16)


def read_log(rows):
    return jnp.sum(rows.astype(f32), axis=0, keepdims=True)


def first_kernel(x_ref, dy_ref, b_ref, c_ref, step_ref, log_ref, packed_ref, xs_ref, dys_ref, cum_ref, cols_ref):
    step = step_ref[...]
    cum = step * -jnp.exp(log_ref[...])
    lane = lax.broadcasted_iota(jnp.int32, cum.shape, 1)
    shift = 1
    while shift < TOKENS:
        cum = cum + jnp.where(lane >= shift, pltpu.roll(cum, shift, 1), 0.0)
        shift *= 2
    cum_ref[...] = cum
    coef = jnp.exp(cum[:, TOKENS - 1 :] - cum) * step
    rows = jnp.concatenate([coef, jnp.exp(cum), cum, step, jnp.zeros((64, TOKENS), f32)], axis=0)
    cols = rows.T
    cols_ref[...] = cols
    b_t = b_ref[...].astype(f32).T.astype(bf16)
    c_t = c_ref[...].astype(f32).T.astype(bf16)
    for k in range(PAIRS):
        at = slice(k * LANES, (k + 1) * LANES)
        xs = (x_ref[:, at].astype(f32) * spread(cols, 0, k)).astype(bf16)
        dys = (dy_ref[:, at].astype(f32) * spread(cols, HEADS, k)).astype(bf16)
        xs_ref[:, at] = xs
        dys_ref[:, at] = dys
        state_in = dot_nn(b_t, xs).astype(bf16)
        state_grad = dot_nn(c_t, dys).astype(bf16)
        logs = log_rows(spread(cols[TOKENS - 1 :], 2 * HEADS, k))
        for j in range(NEAR):
            packed_ref[j, 0:PART, at] = state_in[j * PART : (j + 1) * PART]
            packed_ref[j, PART : 2 * PART, at] = state_grad[j * PART : (j + 1) * PART]
            packed_ref[j, 2 * PART : 2 * PART + 8, at] = logs


def inside_kernel(x_ref, dy_ref, b_ref, c_ref, cum_ref, cols_ref, skip_ref, inner_ref, gb_ref, gc_ref, mix_ref):
    scores = dot_nt(b_ref[...], c_ref[...])
    shape = (TOKENS, TOKENS)
    causal = lax.broadcasted_iota(jnp.int32, shape, 1) >= lax.broadcasted_iota(jnp.int32, shape, 0)
    low = low_lanes()
    low_x = low.astype(f32).astype(bf16)
    high_x = 1 - low_x
    for k in range(PAIRS):
        at = slice(k * LANES, (k + 1) * LANES)
        x = x_ref[:, at]
        dy = dy_ref[:, at]
        found = []
        for half, mask in ((0, low_x), (1, high_x)):
            h = 2 * k + half
            gaps = cum_ref[h : h + 1, :] - cols_ref[:, 2 * HEADS + h : 2 * HEADS + h + 1]
            decay = jnp.exp(jnp.where(causal, gaps, -1e30)) * cols_ref[:, 3 * HEADS + h : 3 * HEADS + h + 1]
            found.append(dot_nn((scores * decay).astype(bf16), dy))
            pairs = dot_nt(x * mask, dy) * decay
            if h == 0:
                mix_ref[...] = pairs
            else:
                mix_ref[...] += pairs
        skip = jnp.where(low, skip_ref[2 * k], skip_ref[2 * k + 1])
        inner_ref[:, at] = jnp.where(low, found[0], found[1]) + skip * dy.astype(f32)
    mix = mix_ref[...].astype(bf16)
    gb_ref[...] = dot_nn(mix, c_ref[...])
    gc_ref[...] = dot_tt(mix, b_ref[...])


def near_totals_kernel(got_ref, out_ref):
    for k in range(PAIRS):
        at = slice(k * LANES, (k + 1) * LANES)
        logs = [read_log(got_ref[m, 2 * PART : 2 * PART + 8, at]) for m in range(NEAR)]
        total = got_ref[0, 0:PART, at].astype(f32)
        for m in range(1, NEAR):
            total = jnp.exp(logs[m]) * total + got_ref[m, 0:PART, at].astype(f32)
        back = got_ref[NEAR - 1, PART : 2 * PART, at].astype(f32)
        for m in reversed(range(NEAR - 1)):
            back = jnp.exp(logs[m]) * back + got_ref[m, PART : 2 * PART, at].astype(f32)
        total, back = total.astype(bf16), back.astype(bf16)
        rows = log_rows(sum(logs[1:], logs[0]))
        for n in range(2):
            out_ref[2 * k + n, 0:HALF] = total[n * HALF : (n + 1) * HALF]
            out_ref[2 * k + n, HALF : 2 * HALF] = back[n * HALF : (n + 1) * HALF]
            out_ref[2 * k + n, 2 * HALF : 2 * HALF + 8] = rows


def far_scan_kernel(got_ref, out_ref):
    decays = [jnp.exp(read_log(got_ref[r, 2 * HALF : 2 * HALF + 8])) for r in range(GROUPS)]
    carry = jnp.zeros((HALF, LANES), f32)
    for r in range(GROUPS):
        out_ref[r, 0:HALF] = carry.astype(bf16)
        carry = decays[r] * carry + got_ref[r, 0:HALF].astype(f32)
    carry = jnp.zeros((HALF, LANES), f32)
    for r in reversed(range(GROUPS)):
        out_ref[r, HALF : 2 * HALF] = carry.astype(bf16)
        carry = decays[r] * carry + got_ref[r, HALF : 2 * HALF].astype(f32)


def near_scan_kernel(carry_ref, got_ref, out_ref):
    for k in range(PAIRS):
        at = slice(k * LANES, (k + 1) * LANES)
        decays = [jnp.exp(read_log(got_ref[m, 2 * PART : 2 * PART + 8, at])) for m in range(NEAR)]
        state = jnp.concatenate([carry_ref[2 * k + n, 0:HALF].astype(f32) for n in range(2)], axis=0)
        for m in range(NEAR):
            out_ref[m, 0:PART, at] = state.astype(bf16)
            state = decays[m] * state + got_ref[m, 0:PART, at].astype(f32)
        state = jnp.concatenate([carry_ref[2 * k + n, HALF : 2 * HALF].astype(f32) for n in range(2)], axis=0)
        for m in reversed(range(NEAR)):
            out_ref[m, PART : 2 * PART, at] = state.astype(bf16)
            state = decays[m] * state + got_ref[m, PART : 2 * PART, at].astype(f32)


def bc_kernel(states_ref, xs_ref, dys_ref, gb_ref, gc_ref, bc_ref, shares_ref):
    start = states_ref[:, 0:PART, :].reshape(STATE, WIDTH)
    end = states_ref[:, PART : 2 * PART, :].reshape(STATE, WIDTH)
    for n, (base, scaled, state) in enumerate(((gb_ref, xs_ref, end), (gc_ref, dys_ref, start))):
        grad = base[...] + dot_nt(scaled[...], state)
        bc_ref[:, n * STATE : (n + 1) * STATE] = grad
        turned = grad.T.astype(bf16)
        for half in range(2):
            for z in range(ZL):
                shares_ref[(2 * n + half) * ZL + z] = turned[half * 64 : (half + 1) * 64]


def input_kernel(states_ref, b_ref, cols_ref, inner_ref, out_ref):
    cols = cols_ref[...]
    for k in range(PAIRS):
        at = slice(k * LANES, (k + 1) * LANES)
        end = states_ref[:, PART : 2 * PART, at].reshape(STATE, LANES)
        carried = dot_nn(b_ref[...], end) * spread(cols, 0, k)
        out_ref[:, at] = (inner_ref[:, at] + carried).astype(bf16)


def weight_kernel(shares_ref, layer_ref, out_ref):
    total = dot_nn(shares_ref[0], layer_ref[0, 0, 0])
    for i in range(1, Y * ZL):
        total += dot_nn(shares_ref[i], layer_ref[i // ZL, 0, i % ZL])
    out_ref[...] = total.astype(bf16)


def call(kernel, outs, flops, exps, **kwargs):
    return pl.pallas_call(
        kernel,
        out_shape=outs if len(outs) > 1 else outs[0],
        compiler_params=pltpu.CompilerParams(vmem_limit_bytes=24 * 1024 * 1024),
        cost_estimate=pl.CostEstimate(flops=flops, bytes_accessed=2 << 20, transcendentals=exps),
        **kwargs,
    )


def shape(dims, dtype):
    return jax.ShapeDtypeStruct(dims, dtype)


def local(head_input, out_grad, b_proj, c_proj, time_step, decay_log, skip_gain, layer_input):
    halves = layer_input.reshape(TOKENS, ZL, 256).transpose(1, 0, 2)
    halves = lax.all_to_all(halves, "zl", 0, 0, tiled=True)
    layer = lax.all_gather(halves, ("y", "x", "core")).reshape(Y, X * CORE, ZL, TOKENS, 256)

    packed, xs, dys, cum, cols = call(
        first_kernel,
        (
            shape((NEAR, 2 * PART + 8, WIDTH), bf16),
            shape((TOKENS, WIDTH), bf16),
            shape((TOKENS, WIDTH), bf16),
            shape((HEADS, TOKENS), f32),
            shape((TOKENS, LANES), f32),
        ),
        1 << 28,
        1 << 13,
    )(head_input, out_grad, b_proj, c_proj, time_step, decay_log.reshape(HEADS, 1))
    near = lax.all_to_all(packed, ("zm", "zl"), 0, 0, tiled=True)

    vmem = pl.BlockSpec(memory_space=pltpu.VMEM)
    inner, grad_b, grad_c = call(
        inside_kernel,
        (shape((TOKENS, WIDTH), f32), shape((TOKENS, STATE), f32), shape((TOKENS, STATE), f32)),
        1 << 30,
        1 << 20,
        in_specs=[vmem] * 6 + [pl.BlockSpec(memory_space=pltpu.SMEM)],
        scratch_shapes=[pltpu.VMEM((TOKENS, TOKENS), f32)],
    )(head_input, out_grad, b_proj, c_proj, cum, cols, skip_gain)

    totals = call(near_totals_kernel, (shape((GROUPS, 2 * HALF + 8, LANES), bf16),), 1 << 18, 1 << 12)(near)
    far = lax.all_to_all(totals, ("y", "zh"), 0, 0, tiled=True)
    carries = call(far_scan_kernel, (shape((GROUPS, 2 * HALF, LANES), bf16),), 1 << 18, 1 << 12)(far)
    carries = lax.all_to_all(carries, ("y", "zh"), 0, 0, tiled=True)
    states = call(near_scan_kernel, (shape((NEAR, 2 * PART, WIDTH), bf16),), 1 << 18, 1 << 12)(carries, near)
    states = lax.all_to_all(states, ("zm", "zl"), 0, 0, tiled=True)

    bc_grad, shares = call(
        bc_kernel, (shape((TOKENS, 2 * STATE), f32), shape((Y * ZL, 64, TOKENS), bf16)), 1 << 27, 0
    )(states, xs, dys, grad_b, grad_c)
    shares = lax.all_to_all(shares, ("y", "zl"), 0, 0, tiled=True)
    input_grad = call(input_kernel, (shape((TOKENS, WIDTH), bf16),), 1 << 27, 0)(states, b_proj, cols, inner)

    term = call(
        weight_kernel,
        (shape((64, X * CORE * 256), bf16),),
        1 << 29,
        0,
        grid=(X * CORE,),
        in_specs=[
            pl.BlockSpec((Y * ZL, 64, TOKENS), lambda g: (0, 0, 0)),
            pl.BlockSpec((Y, 1, ZL, TOKENS, 256), lambda g: (0, g, 0, 0, 0)),
        ],
        out_specs=pl.BlockSpec((64, 256), lambda g: (0, g)),
    )(shares, layer)
    parts = lax.all_to_all(term.reshape(16, 4, X * CORE * 256), ("zh", "zm", "zl"), 0, 0, tiled=True)
    parts = parts.reshape(ZH * ZM, ZL, 4, X * CORE, 256).astype(f32)
    weight = jnp.sum(parts, axis=0).transpose(1, 2, 0, 3).reshape(4, 4096) / (TOKENS * Y * ZH * ZM * ZL)
    return input_grad, bc_grad, weight[None]


def solution(mesh):
    fine = Mesh(mesh.devices.reshape(Y, ZH, ZM, ZL, X, CORE), ("y", "zh", "zm", "zl", "x", "core"))
    seq, head = ("y", "zh", "zm", "zl"), ("x", "core")
    tokens = P(seq, head)
    in_specs = (tokens, tokens, tokens, tokens, P(head, seq), P(head), P(head), tokens)
    out_specs = (tokens, tokens, P(head, seq, None))
    return jax.shard_map(local, mesh=fine, in_specs=in_specs, out_specs=out_specs, check_vma=False)
```

```python
import jax
import jax.numpy as jnp
from jax import lax
from jax.experimental import pallas as pl
from jax.experimental.pallas import tpu as pltpu
from jax.sharding import Mesh, PartitionSpec as P

Y, ZH, ZL, X, CORE = 4, 8, 2, 4, 2
TOKENS = 256
HEADS = 16
PAIRS = 8
STATE = 128
LANES = 128
WIDTH = 1024
BIG = 60 * 1024 * 1024
SMALL = 24 * 1024 * 1024
bf16 = jnp.bfloat16
f32 = jnp.float32


def dot_tt(left, right):
    return lax.dot_general(left, right, (((0,), (0,)), ((), ())), preferred_element_type=f32)


def dot_nt(left, right):
    return lax.dot_general(left, right, (((1,), (1,)), ((), ())), preferred_element_type=f32)


def dot_nn(left, right):
    return lax.dot_general(left, right, (((1,), (0,)), ((), ())), preferred_element_type=f32)


def low_lanes():
    return lax.broadcasted_iota(jnp.int32, (1, LANES), 1) < 64


def spread(columns, first, k):
    return jnp.where(low_lanes(), columns[:, first + 2 * k : first + 2 * k + 1], columns[:, first + 2 * k + 1 : first + 2 * k + 2])


def log_rows(log):
    high = log.astype(bf16).astype(f32)
    mid = (log - high).astype(bf16).astype(f32)
    low = log - high - mid
    row = lax.broadcasted_iota(jnp.int32, (8, log.shape[1]), 0)
    rows = jnp.where(row == 0, high, jnp.where(row == 1, mid, jnp.where(row == 2, low, 0.0)))
    return rows.astype(bf16)


def read_log(rows):
    return jnp.sum(rows.astype(f32), axis=0, keepdims=True)


def start_copies(sources, targets, sems):
    copies = [pltpu.make_async_copy(source, target, sems.at[i]) for i, (source, target) in enumerate(zip(sources, targets))]
    for copy in copies:
        copy.start()
    return copies


def first_kernel(x_hbm, dy_hbm, b_hbm, c_hbm, step_hbm, log_ref, send_ref, keep_ref, xs_ref, dys_ref, cum_ref, cols_ref, x_ref, dy_ref, b_ref, c_ref, step_ref, sems):
    copies = start_copies((step_hbm, b_hbm, c_hbm, x_hbm, dy_hbm), (step_ref, b_ref, c_ref, x_ref, dy_ref), sems)
    copies[0].wait()
    odd = lax.axis_index("zl") == 1
    step = step_ref[...]
    square = (HEADS, HEADS)
    same = lax.broadcasted_iota(jnp.int32, square, 0) == lax.broadcasted_iota(jnp.int32, square, 1)
    rate = jnp.sum(jnp.where(same, jnp.broadcast_to(-jnp.exp(log_ref[...]), square), 0.0), axis=1, keepdims=True)
    cum = step * rate
    lane = lax.broadcasted_iota(jnp.int32, cum.shape, 1)
    shift = 1
    while shift < TOKENS:
        cum = cum + jnp.where(lane >= shift, pltpu.roll(cum, shift, 1), 0.0)
        shift *= 2
    cum_ref[...] = cum
    coef = jnp.exp(cum[:, TOKENS - 1 :] - cum) * step
    rows = jnp.concatenate([coef, jnp.exp(cum), cum, step, jnp.zeros((64, TOKENS), f32)], axis=0)
    cols = rows.T
    cols_ref[...] = cols
    for copy in copies[1:]:
        copy.wait()
    b_t = b_ref[...].astype(f32).T.astype(bf16)
    c_t = c_ref[...].astype(f32).T.astype(bf16)
    for k in range(PAIRS):
        at = slice(k * LANES, (k + 1) * LANES)
        xs = (x_ref[:, at].astype(f32) * spread(cols, 0, k)).astype(bf16)
        dys = (dy_ref[:, at].astype(f32) * spread(cols, HEADS, k)).astype(bf16)
        xs_ref[:, at] = xs
        dys_ref[:, at] = dys
        state_in = dot_nn(b_t, xs)
        state_grad = dot_nn(c_t, dys)
        send_ref[0:STATE, at] = jnp.where(odd, state_grad, state_in).astype(bf16)
        keep_ref[:, at] = jnp.where(odd, state_in, state_grad)
        send_ref[STATE : STATE + 8, at] = log_rows(spread(cols[TOKENS - 1 :], 2 * HEADS, k))


def inside_kernel(x_hbm, dy_hbm, b_hbm, c_hbm, cum_ref, cols_ref, skip_ref, inner_ref, gb_ref, gc_ref, mix_ref, x_ref, dy_ref, b_ref, c_ref, sems):
    copies = start_copies((b_hbm, c_hbm, x_hbm, dy_hbm), (b_ref, c_ref, x_ref, dy_ref), sems)
    for copy in copies:
        copy.wait()
    scores = dot_nt(b_ref[...], c_ref[...])
    shape = (TOKENS, TOKENS)
    causal = lax.broadcasted_iota(jnp.int32, shape, 1) >= lax.broadcasted_iota(jnp.int32, shape, 0)
    low = low_lanes()
    low_x = low.astype(f32).astype(bf16)
    high_x = 1 - low_x
    for k in range(PAIRS):
        at = slice(k * LANES, (k + 1) * LANES)
        x = x_ref[:, at]
        dy = dy_ref[:, at]
        found = []
        for half, mask in ((0, low_x), (1, high_x)):
            h = 2 * k + half
            gaps = cum_ref[h : h + 1, :] - cols_ref[:, 2 * HEADS + h : 2 * HEADS + h + 1]
            decay = jnp.exp(jnp.where(causal, gaps, -1e30)) * cols_ref[:, 3 * HEADS + h : 3 * HEADS + h + 1]
            found.append(dot_nn((scores * decay).astype(bf16), dy))
            pairs = dot_nt(x * mask, dy) * decay
            if h == 0:
                mix_ref[...] = pairs
            else:
                mix_ref[...] += pairs
        skip = jnp.where(low, skip_ref[2 * k], skip_ref[2 * k + 1])
        inner_ref[:, at] = jnp.where(low, found[0], found[1]) + skip * dy.astype(f32)
    mix = mix_ref[...].astype(bf16)
    gb_ref[...] = dot_nn(mix, c_ref[...])
    gc_ref[...] = dot_tt(mix, b_ref[...])


def pair_kernel(send_ref, keep_ref, got_ref, out_ref):
    for k in range(PAIRS):
        at = slice(k * LANES, (k + 1) * LANES)
        own = read_log(send_ref[STATE : STATE + 8, at])
        out_ref[k, 0:STATE] = (keep_ref[:, at] + jnp.exp(own) * got_ref[0:STATE, at].astype(f32)).astype(bf16)
        out_ref[k, STATE : STATE + 8] = log_rows(own + read_log(got_ref[STATE : STATE + 8, at]))


def halves_kernel(layer_ref, other_ref, out_ref):
    columns = pl.ds(pl.multiple_of(lax.axis_index("zl") * 256, 256), 256)
    out_ref[0] = layer_ref[:, columns]
    out_ref[1] = other_ref[:, columns]


def ordered(odd, i, size):
    return odd * i + (1 - odd) * (size - 1 - i)


def total_kernel(got_ref, out_ref):
    odd = lax.axis_index("zl")
    total = jnp.zeros((STATE, LANES), f32)
    for i in range(ZH):
        z = ordered(odd, i, ZH)
        total = jnp.exp(read_log(got_ref[z, STATE : STATE + 8])) * total + got_ref[z, 0:STATE].astype(f32)
    total = total.astype(bf16)
    logs = [read_log(got_ref[z, STATE : STATE + 8]) for z in range(ZH)]
    rows = log_rows(sum(logs[1:], logs[0]))
    for y in range(Y):
        out_ref[y, 0:STATE] = total
        out_ref[y, STATE : STATE + 8] = rows


def scan_kernel(rows_ref, got_ref, out_ref):
    odd = lax.axis_index("zl")
    before = ordered(odd, lax.axis_index("y"), Y)
    state = jnp.zeros((STATE, LANES), f32)
    for i in range(Y - 1):
        y = ordered(odd, i, Y)
        later = jnp.exp(read_log(rows_ref[y, STATE : STATE + 8])) * state + rows_ref[y, 0:STATE].astype(f32)
        state = jnp.where(i < before, later, state)
    for i in range(ZH):
        z = ordered(odd, i, ZH)
        out_ref[z] = state.astype(bf16)
        if i < ZH - 1:
            state = jnp.exp(read_log(got_ref[z, STATE : STATE + 8])) * state + got_ref[z, 0:STATE].astype(f32)


def bc_kernel(carry_ref, other_ref, got_ref, xs_ref, dys_ref, gb_ref, gc_ref, bc_ref, shares_ref, end_ref, start_ref):
    odd = lax.axis_index("zl") == 1
    for k in range(PAIRS):
        at = slice(k * LANES, (k + 1) * LANES)
        decay = jnp.exp(read_log(got_ref[STATE : STATE + 8, at]))
        own = got_ref[0:STATE, at].astype(f32) + decay * carry_ref[k].astype(f32)
        other = other_ref[k].astype(f32)
        start_ref[:, at] = jnp.where(odd, own, other).astype(bf16)
        end_ref[:, at] = jnp.where(odd, other, own).astype(bf16)
    for n, (base, scaled, state) in enumerate(((gb_ref, xs_ref, end_ref), (gc_ref, dys_ref, start_ref))):
        grad = base[...] + dot_nt(scaled[...], state[...])
        bc_ref[:, n * STATE : (n + 1) * STATE] = grad
        turned = grad.T.astype(bf16)
        for half in range(2):
            for z in range(ZL):
                shares_ref[(2 * n + half) * ZL + z] = turned[half * 64 : (half + 1) * 64]


def input_kernel(end_ref, b_ref, cols_ref, inner_ref, out_ref):
    cols = cols_ref[...]
    for k in range(PAIRS):
        at = slice(k * LANES, (k + 1) * LANES)
        carried = dot_nn(b_ref[...], end_ref[:, at]) * spread(cols, 0, k)
        out_ref[:, at] = (inner_ref[:, at] + carried).astype(bf16)


def fetch_kernel(in_ref, out_ref, sem):
    copy = pltpu.make_async_copy(in_ref, out_ref, sem)
    copy.start()
    copy.wait()


def weight_kernel(shares_ref, layer_ref, out_ref):
    odd = lax.axis_index("zl")
    shares = [shares_ref[y * ZL + (odd if z == 0 else 1 - odd)] for y in range(Y) for z in range(ZL)]
    for g in range(X * CORE):
        total = dot_nn(shares[0], layer_ref[0, g, 0])
        for i in range(1, Y * ZL):
            total += dot_nn(shares[i], layer_ref[i // ZL, g, i % ZL])
        out_ref[:, g * 256 : (g + 1) * 256] = total.astype(bf16)


def call(kernel, outs, flops, exps, ins, limit=SMALL, **kwargs):
    return pl.pallas_call(
        kernel,
        out_shape=outs if len(outs) > 1 else outs[0],
        in_specs=ins,
        compiler_params=pltpu.CompilerParams(vmem_limit_bytes=limit),
        cost_estimate=pl.CostEstimate(flops=flops, bytes_accessed=2 << 20, transcendentals=exps),
        **kwargs,
    )


def shape(dims, dtype):
    return jax.ShapeDtypeStruct(dims, dtype)


def local(head_input, out_grad, b_proj, c_proj, time_step, decay_log, skip_gain, layer_input):
    vmem = pl.BlockSpec(memory_space=pltpu.VMEM)
    smem = pl.BlockSpec(memory_space=pltpu.SMEM)
    anywhere = pl.BlockSpec(memory_space=pl.ANY)
    hbm = pl.BlockSpec(memory_space=pltpu.HBM)
    swap = [(0, 1), (1, 0)]
    layer_other = lax.ppermute(layer_input, "zl", swap)

    send, keep, xs, dys, cum, cols = call(
        first_kernel,
        (
            shape((STATE + 8, WIDTH), bf16),
            shape((STATE, WIDTH), f32),
            shape((TOKENS, WIDTH), bf16),
            shape((TOKENS, WIDTH), bf16),
            shape((HEADS, TOKENS), f32),
            shape((TOKENS, LANES), f32),
        ),
        1 << 28,
        1 << 13,
        [hbm] * 5 + [vmem],
        scratch_shapes=[
            pltpu.VMEM((TOKENS, WIDTH), bf16),
            pltpu.VMEM((TOKENS, WIDTH), bf16),
            pltpu.VMEM((TOKENS, STATE), bf16),
            pltpu.VMEM((TOKENS, STATE), bf16),
            pltpu.VMEM((HEADS, TOKENS), f32),
            pltpu.SemaphoreType.DMA((5,)),
        ],
        limit=BIG,
    )(head_input, out_grad, b_proj, c_proj, time_step, decay_log.reshape(1, HEADS))
    send, layer_other = lax.optimization_barrier((send, layer_other))
    got = lax.ppermute(send, "zl", swap)
    halves = call(halves_kernel, (shape((ZL, TOKENS, 256), bf16),), 1 << 10, 0, [vmem] * 2)(
        layer_input, layer_other
    )
    layer = lax.all_gather(halves, ("y", "x", "core")).reshape(Y, X * CORE, ZL, TOKENS, 256)

    pair = call(pair_kernel, (shape((PAIRS, STATE + 8, LANES), bf16),), 1 << 18, 1 << 12, [vmem] * 3, BIG)(send, keep, got)
    far = lax.all_to_all(pair, "zh", 0, 0, tiled=True)

    inner, grad_b, grad_c = call(
        inside_kernel,
        (shape((TOKENS, WIDTH), f32), shape((TOKENS, STATE), f32), shape((TOKENS, STATE), f32)),
        1 << 30,
        1 << 20,
        [hbm] * 4 + [vmem] * 2 + [smem],
        scratch_shapes=[
            pltpu.VMEM((TOKENS, TOKENS), f32),
            pltpu.VMEM((TOKENS, WIDTH), bf16),
            pltpu.VMEM((TOKENS, WIDTH), bf16),
            pltpu.VMEM((TOKENS, STATE), bf16),
            pltpu.VMEM((TOKENS, STATE), bf16),
            pltpu.SemaphoreType.DMA((4,)),
        ],
    )(head_input, out_grad, b_proj, c_proj, cum, cols, skip_gain)

    far, inner, grad_b, grad_c = lax.optimization_barrier((far, inner, grad_b, grad_c))
    rows = call(total_kernel, (shape((Y, STATE + 8, LANES), bf16),), 1 << 18, 1 << 12, [vmem])(far)
    rows = lax.all_to_all(rows, "y", 0, 0, tiled=True)
    carry = call(scan_kernel, (shape((PAIRS, STATE, LANES), bf16),), 1 << 18, 1 << 12, [vmem] * 2)(rows, far)
    carry = lax.all_to_all(carry, "zh", 0, 0, tiled=True)
    other = lax.ppermute(carry, "zl", swap)
    layer = call(
        fetch_kernel,
        (shape(layer.shape, bf16),),
        0,
        0,
        [anywhere],
        out_specs=anywhere,
        scratch_shapes=[pltpu.SemaphoreType.DMA],
    )(layer)
    other, layer = lax.optimization_barrier((other, layer))

    bc_grad, shares, end = call(
        bc_kernel,
        (
            shape((TOKENS, 2 * STATE), f32),
            shape((Y * ZL, 64, TOKENS), bf16),
            shape((STATE, WIDTH), bf16),
        ),
        1 << 27,
        0,
        [vmem] * 7,
        scratch_shapes=[pltpu.VMEM((STATE, WIDTH), bf16)],
    )(carry, other, got, xs, dys, grad_b, grad_c)
    shares = lax.all_to_all(shares, ("y", "zl"), 0, 0, tiled=True)
    input_grad = call(input_kernel, (shape((TOKENS, WIDTH), bf16),), 1 << 27, 0, [vmem] * 4)(end, b_proj, cols, inner)

    term = call(weight_kernel, (shape((64, X * CORE * 256), bf16),), 1 << 29, 0, [vmem] * 2)(shares, layer)
    parts = lax.all_to_all(term.reshape(16, 4, X * CORE * 256), ("zh", "zl"), 0, 0, tiled=True)
    parts = parts.reshape(ZH, ZL, 4, X * CORE, 256).astype(f32)
    weight = jnp.sum(parts, axis=0).transpose(1, 2, 0, 3).reshape(4, 4096) / (TOKENS * Y * ZH * ZL)
    return input_grad, bc_grad, weight[None]


def solution(mesh):
    fine = Mesh(mesh.devices.reshape(Y, ZH, ZL, X, CORE), ("y", "zh", "zl", "x", "core"))
    seq, head = ("y", "zh", "zl"), ("x", "core")
    tokens = P(seq, head)
    in_specs = (tokens, tokens, tokens, tokens, P(head, seq), P(head), P(head), tokens)
    out_specs = (tokens, tokens, P(head, seq, None))
    return jax.shard_map(local, mesh=fine, in_specs=in_specs, out_specs=out_specs, check_vma=False)
```

```python
import jax
import jax.numpy as jnp
from jax import lax
from jax.experimental import pallas as pl
from jax.experimental.pallas import tpu as pltpu
from jax.sharding import Mesh, PartitionSpec as P

Y, ZH, ZL, X, CORE = 4, 8, 2, 4, 2
TOKENS = 256
HEADS = 16
PAIRS = 8
STATE = 128
LANES = 128
WIDTH = 1024
BIG = 60 * 1024 * 1024
SMALL = 24 * 1024 * 1024
bf16 = jnp.bfloat16
f32 = jnp.float32


def dot_tt(left, right):
    return lax.dot_general(left, right, (((0,), (0,)), ((), ())), preferred_element_type=f32)


def dot_nt(left, right):
    return lax.dot_general(left, right, (((1,), (1,)), ((), ())), preferred_element_type=f32)


def dot_nn(left, right):
    return lax.dot_general(left, right, (((1,), (0,)), ((), ())), preferred_element_type=f32)


def low_lanes():
    return lax.broadcasted_iota(jnp.int32, (1, LANES), 1) < 64


def spread(columns, first, k):
    return jnp.where(low_lanes(), columns[:, first + 2 * k : first + 2 * k + 1], columns[:, first + 2 * k + 1 : first + 2 * k + 2])


def log_rows(log):
    high = log.astype(bf16).astype(f32)
    mid = (log - high).astype(bf16).astype(f32)
    low = log - high - mid
    row = lax.broadcasted_iota(jnp.int32, (8, log.shape[1]), 0)
    rows = jnp.where(row == 0, high, jnp.where(row == 1, mid, jnp.where(row == 2, low, 0.0)))
    return rows.astype(bf16)


def read_log(rows):
    return jnp.sum(rows.astype(f32), axis=0, keepdims=True)


def start_copies(sources, targets, sems):
    copies = [pltpu.make_async_copy(source, target, sems.at[i]) for i, (source, target) in enumerate(zip(sources, targets))]
    for copy in copies:
        copy.start()
    return copies


def first_kernel(x_hbm, dy_hbm, b_hbm, c_hbm, step_hbm, log_ref, send_ref, keep_ref, cum_ref, cols_ref, x_ref, dy_ref, b_ref, c_ref, step_ref, sems):
    copies = start_copies((step_hbm, b_hbm, c_hbm, x_hbm, dy_hbm), (step_ref, b_ref, c_ref, x_ref, dy_ref), sems)
    copies[0].wait()
    odd = lax.axis_index("zl") == 1
    step = step_ref[...]
    square = (HEADS, HEADS)
    same = lax.broadcasted_iota(jnp.int32, square, 0) == lax.broadcasted_iota(jnp.int32, square, 1)
    rate = jnp.sum(jnp.where(same, jnp.broadcast_to(-jnp.exp(log_ref[...]), square), 0.0), axis=1, keepdims=True)
    cum = step * rate
    lane = lax.broadcasted_iota(jnp.int32, cum.shape, 1)
    shift = 1
    while shift < TOKENS:
        cum = cum + jnp.where(lane >= shift, pltpu.roll(cum, shift, 1), 0.0)
        shift *= 2
    cum_ref[...] = cum
    coef = jnp.exp(cum[:, TOKENS - 1 :] - cum) * step
    rows = jnp.concatenate([coef, jnp.exp(cum), cum, step, jnp.zeros((64, TOKENS), f32)], axis=0)
    cols = rows.T
    cols_ref[...] = cols
    for copy in copies[1:]:
        copy.wait()
    b_t = b_ref[...].astype(f32).T.astype(bf16)
    c_t = c_ref[...].astype(f32).T.astype(bf16)
    for k in range(PAIRS):
        at = slice(k * LANES, (k + 1) * LANES)
        xs = (x_ref[:, at].astype(f32) * spread(cols, 0, k)).astype(bf16)
        dys = (dy_ref[:, at].astype(f32) * spread(cols, HEADS, k)).astype(bf16)
        state_in = dot_nn(b_t, xs)
        state_grad = dot_nn(c_t, dys)
        send_ref[0:STATE, at] = jnp.where(odd, state_grad, state_in).astype(bf16)
        keep_ref[0:STATE, at] = jnp.where(odd, state_in, state_grad)
        log = spread(cols[TOKENS - 1 :], 2 * HEADS, k)
        send_ref[STATE : STATE + 8, at] = log_rows(log)
        keep_ref[STATE : STATE + 8, at] = jnp.broadcast_to(log, (8, LANES))


def inside_kernel(x_hbm, dy_hbm, b_hbm, c_hbm, cum_ref, cols_ref, skip_ref, inner_ref, gb_ref, gc_ref, xs_ref, dys_ref, mix_ref, x_ref, dy_ref, b_ref, c_ref, sems):
    copies = start_copies((b_hbm, c_hbm, x_hbm, dy_hbm), (b_ref, c_ref, x_ref, dy_ref), sems)
    for copy in copies:
        copy.wait()
    scores = dot_nt(b_ref[...], c_ref[...])
    shape = (TOKENS, TOKENS)
    causal = lax.broadcasted_iota(jnp.int32, shape, 1) >= lax.broadcasted_iota(jnp.int32, shape, 0)
    low = low_lanes()
    low_x = low.astype(f32).astype(bf16)
    high_x = 1 - low_x
    for k in range(PAIRS):
        at = slice(k * LANES, (k + 1) * LANES)
        x = x_ref[:, at]
        dy = dy_ref[:, at]
        xs_ref[:, at] = (x.astype(f32) * spread(cols_ref, 0, k)).astype(bf16)
        dys_ref[:, at] = (dy.astype(f32) * spread(cols_ref, HEADS, k)).astype(bf16)
        found = []
        for half, mask in ((0, low_x), (1, high_x)):
            h = 2 * k + half
            gaps = cum_ref[h : h + 1, :] - cols_ref[:, 2 * HEADS + h : 2 * HEADS + h + 1]
            decay = jnp.exp(jnp.where(causal, gaps, -1e30)) * cols_ref[:, 3 * HEADS + h : 3 * HEADS + h + 1]
            found.append(dot_nn((scores * decay).astype(bf16), dy))
            pairs = dot_nt(x * mask, dy) * decay
            if h == 0:
                mix_ref[...] = pairs
            else:
                mix_ref[...] += pairs
        skip = jnp.where(low, skip_ref[2 * k], skip_ref[2 * k + 1])
        inner_ref[:, at] = jnp.where(low, found[0], found[1]) + skip * dy.astype(f32)
    mix = mix_ref[...].astype(bf16)
    gb_ref[...] = dot_nn(mix, c_ref[...])
    gc_ref[...] = dot_tt(mix, b_ref[...])


def pair_kernel(keep_ref, got_ref, out_ref):
    for k in range(PAIRS):
        at = slice(k * LANES, (k + 1) * LANES)
        own = keep_ref[STATE : STATE + 1, at]
        out_ref[k, 0:STATE] = (keep_ref[0:STATE, at] + jnp.exp(own) * got_ref[0:STATE, at].astype(f32)).astype(bf16)
        out_ref[k, STATE : STATE + 8] = log_rows(own + read_log(got_ref[STATE : STATE + 8, at]))


def halves_kernel(layer_ref, other_ref, out_ref):
    columns = pl.ds(pl.multiple_of(lax.axis_index("zl") * 256, 256), 256)
    out_ref[0] = layer_ref[:, columns]
    out_ref[1] = other_ref[...]


def ordered(odd, i, size):
    return odd * i + (1 - odd) * (size - 1 - i)


def total_kernel(got_ref, out_ref):
    odd = lax.axis_index("zl")
    total = jnp.zeros((STATE, LANES), f32)
    for i in range(ZH):
        z = ordered(odd, i, ZH)
        total = jnp.exp(read_log(got_ref[z, STATE : STATE + 8])) * total + got_ref[z, 0:STATE].astype(f32)
    total = total.astype(bf16)
    logs = [read_log(got_ref[z, STATE : STATE + 8]) for z in range(ZH)]
    rows = log_rows(sum(logs[1:], logs[0]))
    for y in range(Y):
        out_ref[y, 0:STATE] = total
        out_ref[y, STATE : STATE + 8] = rows


def scan_kernel(rows_ref, got_ref, out_ref):
    odd = lax.axis_index("zl")
    before = ordered(odd, lax.axis_index("y"), Y)
    state = jnp.zeros((STATE, LANES), f32)
    for i in range(Y - 1):
        y = ordered(odd, i, Y)
        later = jnp.exp(read_log(rows_ref[y, STATE : STATE + 8])) * state + rows_ref[y, 0:STATE].astype(f32)
        state = jnp.where(i < before, later, state)
    for i in range(ZH):
        z = ordered(odd, i, ZH)
        out_ref[z] = state.astype(bf16)
        if i < ZH - 1:
            state = jnp.exp(read_log(got_ref[z, STATE : STATE + 8])) * state + got_ref[z, 0:STATE].astype(f32)


def bc_kernel(carry_ref, other_ref, got_ref, xs_ref, dys_ref, gb_ref, gc_ref, bc_ref, shares_ref, end_ref, start_ref):
    odd = lax.axis_index("zl") == 1
    for k in range(PAIRS):
        at = slice(k * LANES, (k + 1) * LANES)
        decay = jnp.exp(read_log(got_ref[STATE : STATE + 8, at]))
        own = got_ref[0:STATE, at].astype(f32) + decay * carry_ref[k].astype(f32)
        other = other_ref[k].astype(f32)
        start_ref[:, at] = jnp.where(odd, own, other).astype(bf16)
        end_ref[:, at] = jnp.where(odd, other, own).astype(bf16)
    for n, (base, scaled, state) in enumerate(((gb_ref, xs_ref, end_ref), (gc_ref, dys_ref, start_ref))):
        grad = base[...] + dot_nt(scaled[...], state[...])
        bc_ref[:, n * STATE : (n + 1) * STATE] = grad
        turned = grad.T.astype(bf16)
        for half in range(2):
            for z in range(ZL):
                shares_ref[(2 * n + half) * ZL + z] = turned[half * 64 : (half + 1) * 64]


def input_kernel(end_ref, b_ref, cols_ref, inner_ref, out_ref):
    cols = cols_ref[...]
    for k in range(PAIRS):
        at = slice(k * LANES, (k + 1) * LANES)
        carried = dot_nn(b_ref[...], end_ref[:, at]) * spread(cols, 0, k)
        out_ref[:, at] = (inner_ref[:, at] + carried).astype(bf16)


def fetch_kernel(in_ref, out_ref, sem):
    copy = pltpu.make_async_copy(in_ref, out_ref, sem)
    copy.start()
    copy.wait()


def fetch(array):
    anywhere = pl.BlockSpec(memory_space=pl.ANY)
    return call(
        fetch_kernel,
        (shape(array.shape, array.dtype),),
        0,
        0,
        [anywhere],
        out_specs=anywhere,
        scratch_shapes=[pltpu.SemaphoreType.DMA],
    )(array)


def weight_kernel(shares_ref, layer_ref, out_ref):
    odd = lax.axis_index("zl")
    shares = [shares_ref[y * ZL + (odd if z == 0 else 1 - odd)] for y in range(Y) for z in range(ZL)]
    for g in range(X * CORE):
        total = dot_nn(shares[0], layer_ref[0, g, 0])
        for i in range(1, Y * ZL):
            total += dot_nn(shares[i], layer_ref[i // ZL, g, i % ZL])
        for z in range(ZH * ZL):
            out_ref[z, :, g * 256 : (g + 1) * 256] = total[4 * z : 4 * z + 4].astype(bf16)


def sum_kernel(parts_ref, out_ref):
    for g in range(X * CORE):
        at = slice(g * 256, (g + 1) * 256)
        for z in range(ZL):
            total = parts_ref[z, :, at].astype(f32)
            for i in range(1, ZH):
                total += parts_ref[ZL * i + z, :, at].astype(f32)
            first = (g * ZL + z) * 256
            out_ref[:, first : first + 256] = total * (1.0 / (TOKENS * Y * ZH * ZL))


def call(kernel, outs, flops, exps, ins, limit=SMALL, **kwargs):
    return pl.pallas_call(
        kernel,
        out_shape=outs if len(outs) > 1 else outs[0],
        in_specs=ins,
        compiler_params=pltpu.CompilerParams(vmem_limit_bytes=limit),
        cost_estimate=pl.CostEstimate(flops=flops, bytes_accessed=2 << 20, transcendentals=exps),
        **kwargs,
    )


def shape(dims, dtype):
    return jax.ShapeDtypeStruct(dims, dtype)


def local(head_input, out_grad, b_proj, c_proj, time_step, decay_log, skip_gain, layer_input):
    vmem = pl.BlockSpec(memory_space=pltpu.VMEM)
    smem = pl.BlockSpec(memory_space=pltpu.SMEM)
    hbm = pl.BlockSpec(memory_space=pltpu.HBM)
    swap = [(0, 1), (1, 0)]
    away = lax.dynamic_slice_in_dim(layer_input, (1 - lax.axis_index("zl")) * 256, 256, 1)
    layer_other = lax.ppermute(away, "zl", swap)

    send, keep, cum, cols = call(
        first_kernel,
        (
            shape((STATE + 8, WIDTH), bf16),
            shape((STATE + 8, WIDTH), f32),
            shape((HEADS, TOKENS), f32),
            shape((TOKENS, LANES), f32),
        ),
        1 << 28,
        1 << 13,
        [hbm] * 5 + [vmem],
        scratch_shapes=[
            pltpu.VMEM((TOKENS, WIDTH), bf16),
            pltpu.VMEM((TOKENS, WIDTH), bf16),
            pltpu.VMEM((TOKENS, STATE), bf16),
            pltpu.VMEM((TOKENS, STATE), bf16),
            pltpu.VMEM((HEADS, TOKENS), f32),
            pltpu.SemaphoreType.DMA((5,)),
        ],
        limit=BIG,
    )(head_input, out_grad, b_proj, c_proj, time_step, decay_log.reshape(1, HEADS))
    send, layer_other = lax.optimization_barrier((send, layer_other))
    got = lax.ppermute(send, "zl", swap)
    halves = call(halves_kernel, (shape((ZL, TOKENS, 256), bf16),), 1 << 10, 0, [vmem] * 2)(
        layer_input, layer_other
    )
    layer = lax.all_gather(halves, ("y", "x", "core")).reshape(Y, X * CORE, ZL, TOKENS, 256)

    got, keep = lax.optimization_barrier((got, fetch(keep)))
    pair = call(pair_kernel, (shape((PAIRS, STATE + 8, LANES), bf16),), 1 << 18, 1 << 12, [vmem] * 2)(keep, got)
    far = lax.all_to_all(pair, "zh", 0, 0, tiled=True)

    inner, grad_b, grad_c, xs, dys = call(
        inside_kernel,
        (
            shape((TOKENS, WIDTH), f32),
            shape((TOKENS, STATE), f32),
            shape((TOKENS, STATE), f32),
            shape((TOKENS, WIDTH), bf16),
            shape((TOKENS, WIDTH), bf16),
        ),
        1 << 30,
        1 << 20,
        [hbm] * 4 + [vmem] * 2 + [smem],
        scratch_shapes=[
            pltpu.VMEM((TOKENS, TOKENS), f32),
            pltpu.VMEM((TOKENS, WIDTH), bf16),
            pltpu.VMEM((TOKENS, WIDTH), bf16),
            pltpu.VMEM((TOKENS, STATE), bf16),
            pltpu.VMEM((TOKENS, STATE), bf16),
            pltpu.SemaphoreType.DMA((4,)),
        ],
    )(head_input, out_grad, b_proj, c_proj, cum, cols, skip_gain)

    far, inner, grad_b, grad_c, xs, dys = lax.optimization_barrier((far, inner, grad_b, grad_c, xs, dys))
    rows = call(total_kernel, (shape((Y, STATE + 8, LANES), bf16),), 1 << 18, 1 << 12, [vmem])(far)
    rows = lax.all_to_all(rows, "y", 0, 0, tiled=True)
    carry = call(scan_kernel, (shape((PAIRS, STATE, LANES), bf16),), 1 << 18, 1 << 12, [vmem] * 2)(rows, far)
    carry = lax.all_to_all(carry, "zh", 0, 0, tiled=True)
    other = lax.ppermute(carry, "zl", swap)
    layer = fetch(layer)
    other, layer = lax.optimization_barrier((other, layer))

    bc_grad, shares, end = call(
        bc_kernel,
        (
            shape((TOKENS, 2 * STATE), f32),
            shape((Y * ZL, 64, TOKENS), bf16),
            shape((STATE, WIDTH), bf16),
        ),
        1 << 27,
        0,
        [vmem] * 7,
        scratch_shapes=[pltpu.VMEM((STATE, WIDTH), bf16)],
    )(carry, other, got, xs, dys, grad_b, grad_c)
    shares = lax.all_to_all(shares, ("y", "zl"), 0, 0, tiled=True)
    input_grad = call(input_kernel, (shape((TOKENS, WIDTH), bf16),), 1 << 27, 0, [vmem] * 4)(end, b_proj, cols, inner)

    term = call(weight_kernel, (shape((ZH * ZL, 4, X * CORE * 256), bf16),), 1 << 29, 0, [vmem] * 2)(shares, layer)
    parts = lax.all_to_all(term, ("zh", "zl"), 0, 0, tiled=True)
    weight = call(sum_kernel, (shape((4, X * CORE * ZL * 256), f32),), 1 << 18, 0, [vmem])(parts)
    return input_grad, bc_grad, weight[None]


def solution(mesh):
    fine = Mesh(mesh.devices.reshape(Y, ZH, ZL, X, CORE), ("y", "zh", "zl", "x", "core"))
    seq, head = ("y", "zh", "zl"), ("x", "core")
    tokens = P(seq, head)
    in_specs = (tokens, tokens, tokens, tokens, P(head, seq), P(head), P(head), tokens)
    out_specs = (tokens, tokens, P(head, seq, None))
    return jax.shard_map(local, mesh=fine, in_specs=in_specs, out_specs=out_specs, check_vma=False)
```

```python
import jax
import jax.numpy as jnp
from jax import lax
from jax.experimental import pallas as pl
from jax.experimental.pallas import tpu as pltpu
from jax.sharding import Mesh, PartitionSpec as P

Y, ZH, ZL, X, CORE = 4, 8, 2, 4, 2
TOKENS = 256
HEADS = 16
PAIRS = 8
STATE = 128
LANES = 128
WIDTH = 1024
BIG = 60 * 1024 * 1024
SMALL = 24 * 1024 * 1024
bf16 = jnp.bfloat16
f32 = jnp.float32


def dot_tt(left, right):
    return lax.dot_general(left, right, (((0,), (0,)), ((), ())), preferred_element_type=f32)


def dot_nt(left, right):
    return lax.dot_general(left, right, (((1,), (1,)), ((), ())), preferred_element_type=f32)


def dot_nn(left, right):
    return lax.dot_general(left, right, (((1,), (0,)), ((), ())), preferred_element_type=f32)


def low_lanes():
    return lax.broadcasted_iota(jnp.int32, (1, LANES), 1) < 64


def spread(columns, first, k):
    return jnp.where(low_lanes(), columns[:, first + 2 * k : first + 2 * k + 1], columns[:, first + 2 * k + 1 : first + 2 * k + 2])


def log_rows(log):
    high = log.astype(bf16).astype(f32)
    mid = (log - high).astype(bf16).astype(f32)
    low = log - high - mid
    row = lax.broadcasted_iota(jnp.int32, (8, log.shape[1]), 0)
    rows = jnp.where(row == 0, high, jnp.where(row == 1, mid, jnp.where(row == 2, low, 0.0)))
    return rows.astype(bf16)


def read_log(rows):
    return jnp.sum(rows.astype(f32), axis=0, keepdims=True)


def start_copies(sources, targets, sems):
    copies = [pltpu.make_async_copy(source, target, sems.at[i]) for i, (source, target) in enumerate(zip(sources, targets))]
    for copy in copies:
        copy.start()
    return copies


def first_kernel(x_hbm, dy_hbm, b_hbm, c_hbm, step_hbm, log_ref, send_ref, keep_ref, cum_ref, cols_ref, x_ref, dy_ref, b_ref, c_ref, step_ref, sems):
    copies = start_copies((step_hbm, b_hbm, c_hbm, x_hbm, dy_hbm), (step_ref, b_ref, c_ref, x_ref, dy_ref), sems)
    copies[0].wait()
    odd = lax.axis_index("zl") == 1
    step = step_ref[...]
    square = (HEADS, HEADS)
    same = lax.broadcasted_iota(jnp.int32, square, 0) == lax.broadcasted_iota(jnp.int32, square, 1)
    rate = jnp.sum(jnp.where(same, jnp.broadcast_to(-jnp.exp(log_ref[...]), square), 0.0), axis=1, keepdims=True)
    cum = step * rate
    lane = lax.broadcasted_iota(jnp.int32, cum.shape, 1)
    shift = 1
    while shift < TOKENS:
        cum = cum + jnp.where(lane >= shift, pltpu.roll(cum, shift, 1), 0.0)
        shift *= 2
    cum_ref[...] = cum
    coef = jnp.exp(cum[:, TOKENS - 1 :] - cum) * step
    rows = jnp.concatenate([coef, jnp.exp(cum), cum, step, jnp.zeros((64, TOKENS), f32)], axis=0)
    cols = rows.T
    cols_ref[...] = cols
    for copy in copies[1:]:
        copy.wait()
    b_t = b_ref[...].astype(f32).T.astype(bf16)
    c_t = c_ref[...].astype(f32).T.astype(bf16)
    for k in range(PAIRS):
        at = slice(k * LANES, (k + 1) * LANES)
        xs = (x_ref[:, at].astype(f32) * spread(cols, 0, k)).astype(bf16)
        dys = (dy_ref[:, at].astype(f32) * spread(cols, HEADS, k)).astype(bf16)
        state_in = dot_nn(b_t, xs)
        state_grad = dot_nn(c_t, dys)
        send_ref[0:STATE, at] = jnp.where(odd, state_grad, state_in).astype(bf16)
        keep_ref[0:STATE, at] = jnp.where(odd, state_in, state_grad)
        log = spread(cols[TOKENS - 1 :], 2 * HEADS, k)
        send_ref[STATE : STATE + 8, at] = log_rows(log)
        keep_ref[STATE : STATE + 8, at] = jnp.broadcast_to(log, (8, LANES))


def inside_kernel(x_hbm, dy_hbm, b_hbm, c_hbm, cum_ref, cols_ref, skip_ref, inner_ref, gb_ref, gc_ref, xs_ref, dys_ref, mix_ref, x_ref, dy_ref, b_ref, c_ref, sems):
    copies = start_copies((b_hbm, c_hbm, x_hbm, dy_hbm), (b_ref, c_ref, x_ref, dy_ref), sems)
    for copy in copies:
        copy.wait()
    scores = dot_nt(b_ref[...], c_ref[...])
    shape = (TOKENS, TOKENS)
    causal = lax.broadcasted_iota(jnp.int32, shape, 1) >= lax.broadcasted_iota(jnp.int32, shape, 0)
    low = low_lanes()
    low_x = low.astype(f32).astype(bf16)
    high_x = 1 - low_x
    for k in range(PAIRS):
        at = slice(k * LANES, (k + 1) * LANES)
        x = x_ref[:, at]
        dy = dy_ref[:, at]
        xs_ref[:, at] = (x.astype(f32) * spread(cols_ref, 0, k)).astype(bf16)
        dys_ref[:, at] = (dy.astype(f32) * spread(cols_ref, HEADS, k)).astype(bf16)
        found = []
        for half, mask in ((0, low_x), (1, high_x)):
            h = 2 * k + half
            gaps = cum_ref[h : h + 1, :] - cols_ref[:, 2 * HEADS + h : 2 * HEADS + h + 1]
            decay = jnp.exp(jnp.where(causal, gaps, -1e30)) * cols_ref[:, 3 * HEADS + h : 3 * HEADS + h + 1]
            found.append(dot_nn((scores * decay).astype(bf16), dy))
            pairs = dot_nt(x * mask, dy) * decay
            if h == 0:
                mix_ref[...] = pairs
            else:
                mix_ref[...] += pairs
        skip = jnp.where(low, skip_ref[2 * k], skip_ref[2 * k + 1])
        inner_ref[:, at] = jnp.where(low, found[0], found[1]) + skip * dy.astype(f32)
    mix = mix_ref[...].astype(bf16)
    gb_ref[...] = dot_nn(mix, c_ref[...])
    gc_ref[...] = dot_tt(mix, b_ref[...])


def pair_kernel(keep_ref, got_ref, out_ref):
    for k in range(PAIRS):
        at = slice(k * LANES, (k + 1) * LANES)
        own = keep_ref[STATE : STATE + 1, at]
        out_ref[k, 0:STATE] = (keep_ref[0:STATE, at] + jnp.exp(own) * got_ref[0:STATE, at].astype(f32)).astype(bf16)
        out_ref[k, STATE : STATE + 8] = log_rows(own + read_log(got_ref[STATE : STATE + 8, at]))


def halves_kernel(layer_ref, other_ref, out_ref):
    columns = pl.ds(pl.multiple_of(lax.axis_index("zl") * 256, 256), 256)
    out_ref[0] = layer_ref[:, columns]
    out_ref[1] = other_ref[...]


def ordered(odd, i, size):
    return odd * i + (1 - odd) * (size - 1 - i)


def total_kernel(got_ref, out_ref):
    odd = lax.axis_index("zl")
    total = jnp.zeros((STATE, LANES), f32)
    for i in range(ZH):
        z = ordered(odd, i, ZH)
        total = jnp.exp(read_log(got_ref[z, STATE : STATE + 8])) * total + got_ref[z, 0:STATE].astype(f32)
    total = total.astype(bf16)
    logs = [read_log(got_ref[z, STATE : STATE + 8]) for z in range(ZH)]
    rows = log_rows(sum(logs[1:], logs[0]))
    for y in range(Y):
        out_ref[y, 0:STATE] = total
        out_ref[y, STATE : STATE + 8] = rows


def scan_kernel(rows_ref, got_ref, out_ref):
    odd = lax.axis_index("zl")
    before = ordered(odd, lax.axis_index("y"), Y)
    state = jnp.zeros((STATE, LANES), f32)
    for i in range(Y - 1):
        y = ordered(odd, i, Y)
        later = jnp.exp(read_log(rows_ref[y, STATE : STATE + 8])) * state + rows_ref[y, 0:STATE].astype(f32)
        state = jnp.where(i < before, later, state)
    for i in range(ZH):
        z = ordered(odd, i, ZH)
        out_ref[z] = state.astype(bf16)
        if i < ZH - 1:
            state = jnp.exp(read_log(got_ref[z, STATE : STATE + 8])) * state + got_ref[z, 0:STATE].astype(f32)


def own_kernel(carry_ref, got_ref, xs_ref, dys_ref, gb_ref, gc_ref, own_ref, grad_ref):
    odd = lax.axis_index("zl") == 1
    for k in range(PAIRS):
        at = slice(k * LANES, (k + 1) * LANES)
        decay = jnp.exp(read_log(got_ref[STATE : STATE + 8, at]))
        own_ref[:, at] = (got_ref[0:STATE, at].astype(f32) + decay * carry_ref[k].astype(f32)).astype(bf16)

    @pl.when(odd)
    def _():
        grad_ref[...] = gc_ref[...] + dot_nt(dys_ref[...], own_ref[...])

    @pl.when(jnp.logical_not(odd))
    def _():
        grad_ref[...] = gb_ref[...] + dot_nt(xs_ref[...], own_ref[...])


def bc_kernel(other_ref, own_ref, grad_ref, xs_ref, dys_ref, gb_ref, gc_ref, bc_ref, shares_ref, end_ref, state_ref):
    odd = lax.axis_index("zl") == 1
    for k in range(PAIRS):
        state_ref[:, k * LANES : (k + 1) * LANES] = other_ref[k]

    def finish(grad_b, grad_c, end):
        end_ref[...] = end[...]
        for n, grad in enumerate((grad_b, grad_c)):
            bc_ref[:, n * STATE : (n + 1) * STATE] = grad
            turned = grad.T.astype(bf16)
            for half in range(2):
                for z in range(ZL):
                    shares_ref[(2 * n + half) * ZL + z] = turned[half * 64 : (half + 1) * 64]

    @pl.when(odd)
    def _():
        finish(gb_ref[...] + dot_nt(xs_ref[...], state_ref[...]), grad_ref[...], state_ref)

    @pl.when(jnp.logical_not(odd))
    def _():
        finish(grad_ref[...], gc_ref[...] + dot_nt(dys_ref[...], state_ref[...]), own_ref)


def input_kernel(end_ref, b_ref, cols_ref, inner_ref, out_ref):
    cols = cols_ref[...]
    for k in range(PAIRS):
        at = slice(k * LANES, (k + 1) * LANES)
        carried = dot_nn(b_ref[...], end_ref[:, at]) * spread(cols, 0, k)
        out_ref[:, at] = (inner_ref[:, at] + carried).astype(bf16)


def fetch_kernel(in_ref, out_ref, sem):
    copy = pltpu.make_async_copy(in_ref, out_ref, sem)
    copy.start()
    copy.wait()


def fetch(array):
    anywhere = pl.BlockSpec(memory_space=pl.ANY)
    return call(
        fetch_kernel,
        (shape(array.shape, array.dtype),),
        0,
        0,
        [anywhere],
        out_specs=anywhere,
        scratch_shapes=[pltpu.SemaphoreType.DMA],
    )(array)


def weight_kernel(shares_ref, layer_ref, out_ref):
    odd = lax.axis_index("zl")
    shares = [shares_ref[y * ZL + (odd if z == 0 else 1 - odd)] for y in range(Y) for z in range(ZL)]
    for g in range(X * CORE):
        total = dot_nn(shares[0], layer_ref[0, g, 0])
        for i in range(1, Y * ZL):
            total += dot_nn(shares[i], layer_ref[i // ZL, g, i % ZL])
        for z in range(ZH * ZL):
            out_ref[z, :, g * 256 : (g + 1) * 256] = total[4 * z : 4 * z + 4].astype(bf16)


def sum_kernel(parts_ref, out_ref):
    for g in range(X * CORE):
        at = slice(g * 256, (g + 1) * 256)
        for z in range(ZL):
            total = parts_ref[z, :, at].astype(f32)
            for i in range(1, ZH):
                total += parts_ref[ZL * i + z, :, at].astype(f32)
            first = (g * ZL + z) * 256
            out_ref[:, first : first + 256] = total * (1.0 / (TOKENS * Y * ZH * ZL))


def call(kernel, outs, flops, exps, ins, limit=SMALL, **kwargs):
    return pl.pallas_call(
        kernel,
        out_shape=outs if len(outs) > 1 else outs[0],
        in_specs=ins,
        compiler_params=pltpu.CompilerParams(vmem_limit_bytes=limit),
        cost_estimate=pl.CostEstimate(flops=flops, bytes_accessed=2 << 20, transcendentals=exps),
        **kwargs,
    )


def shape(dims, dtype):
    return jax.ShapeDtypeStruct(dims, dtype)


def local(head_input, out_grad, b_proj, c_proj, time_step, decay_log, skip_gain, layer_input):
    vmem = pl.BlockSpec(memory_space=pltpu.VMEM)
    smem = pl.BlockSpec(memory_space=pltpu.SMEM)
    hbm = pl.BlockSpec(memory_space=pltpu.HBM)
    swap = [(0, 1), (1, 0)]
    away = lax.dynamic_slice_in_dim(layer_input, (1 - lax.axis_index("zl")) * 256, 256, 1)
    layer_other = lax.ppermute(away, "zl", swap)

    send, keep, cum, cols = call(
        first_kernel,
        (
            shape((STATE + 8, WIDTH), bf16),
            shape((STATE + 8, WIDTH), f32),
            shape((HEADS, TOKENS), f32),
            shape((TOKENS, LANES), f32),
        ),
        1 << 28,
        1 << 13,
        [hbm] * 5 + [vmem],
        scratch_shapes=[
            pltpu.VMEM((TOKENS, WIDTH), bf16),
            pltpu.VMEM((TOKENS, WIDTH), bf16),
            pltpu.VMEM((TOKENS, STATE), bf16),
            pltpu.VMEM((TOKENS, STATE), bf16),
            pltpu.VMEM((HEADS, TOKENS), f32),
            pltpu.SemaphoreType.DMA((5,)),
        ],
        limit=BIG,
    )(head_input, out_grad, b_proj, c_proj, time_step, decay_log.reshape(1, HEADS))
    send, layer_other = lax.optimization_barrier((send, layer_other))
    got = lax.ppermute(send, "zl", swap)
    halves = call(halves_kernel, (shape((ZL, TOKENS, 256), bf16),), 1 << 10, 0, [vmem] * 2)(
        layer_input, layer_other
    )
    layer = lax.all_gather(halves, ("y", "x", "core")).reshape(Y, X * CORE, ZL, TOKENS, 256)

    got, keep = lax.optimization_barrier((got, fetch(keep)))
    pair = call(pair_kernel, (shape((PAIRS, STATE + 8, LANES), bf16),), 1 << 18, 1 << 12, [vmem] * 2)(keep, got)
    far = lax.all_to_all(pair, "zh", 0, 0, tiled=True)

    inner, grad_b, grad_c, xs, dys = call(
        inside_kernel,
        (
            shape((TOKENS, WIDTH), f32),
            shape((TOKENS, STATE), f32),
            shape((TOKENS, STATE), f32),
            shape((TOKENS, WIDTH), bf16),
            shape((TOKENS, WIDTH), bf16),
        ),
        1 << 30,
        1 << 20,
        [hbm] * 4 + [vmem] * 2 + [smem],
        scratch_shapes=[
            pltpu.VMEM((TOKENS, TOKENS), f32),
            pltpu.VMEM((TOKENS, WIDTH), bf16),
            pltpu.VMEM((TOKENS, WIDTH), bf16),
            pltpu.VMEM((TOKENS, STATE), bf16),
            pltpu.VMEM((TOKENS, STATE), bf16),
            pltpu.SemaphoreType.DMA((4,)),
        ],
    )(head_input, out_grad, b_proj, c_proj, cum, cols, skip_gain)

    far, inner, grad_b, grad_c, xs, dys = lax.optimization_barrier((far, inner, grad_b, grad_c, xs, dys))
    rows = call(total_kernel, (shape((Y, STATE + 8, LANES), bf16),), 1 << 18, 1 << 12, [vmem])(far)
    rows = lax.all_to_all(rows, "y", 0, 0, tiled=True)
    carry = call(scan_kernel, (shape((PAIRS, STATE, LANES), bf16),), 1 << 18, 1 << 12, [vmem] * 2)(rows, far)
    carry = lax.all_to_all(carry, "zh", 0, 0, tiled=True)
    other = lax.ppermute(carry, "zl", swap)
    layer = fetch(layer)
    own, grad = call(
        own_kernel, (shape((STATE, WIDTH), bf16), shape((TOKENS, STATE), f32)), 1 << 26, 0, [vmem] * 6
    )(carry, got, xs, dys, grad_b, grad_c)
    other, layer, own, grad = lax.optimization_barrier((other, layer, own, grad))

    bc_grad, shares, end = call(
        bc_kernel,
        (
            shape((TOKENS, 2 * STATE), f32),
            shape((Y * ZL, 64, TOKENS), bf16),
            shape((STATE, WIDTH), bf16),
        ),
        1 << 27,
        0,
        [vmem] * 7,
        scratch_shapes=[pltpu.VMEM((STATE, WIDTH), bf16)],
    )(other, own, grad, xs, dys, grad_b, grad_c)
    shares = lax.all_to_all(shares, ("y", "zl"), 0, 0, tiled=True)
    input_grad = call(input_kernel, (shape((TOKENS, WIDTH), bf16),), 1 << 27, 0, [vmem] * 4)(end, b_proj, cols, inner)

    term = call(weight_kernel, (shape((ZH * ZL, 4, X * CORE * 256), bf16),), 1 << 29, 0, [vmem] * 2)(shares, layer)
    parts = lax.all_to_all(term, ("zh", "zl"), 0, 0, tiled=True)
    weight = call(sum_kernel, (shape((4, X * CORE * ZL * 256), f32),), 1 << 18, 0, [vmem])(parts)
    return input_grad, bc_grad, weight[None]


def solution(mesh):
    fine = Mesh(mesh.devices.reshape(Y, ZH, ZL, X, CORE), ("y", "zh", "zl", "x", "core"))
    seq, head = ("y", "zh", "zl"), ("x", "core")
    tokens = P(seq, head)
    in_specs = (tokens, tokens, tokens, tokens, P(head, seq), P(head), P(head), tokens)
    out_specs = (tokens, tokens, P(head, seq, None))
    return jax.shard_map(local, mesh=fine, in_specs=in_specs, out_specs=out_specs, check_vma=False)
```
